768 devices in a mesh: dp: 12 (over z), mp: 64 (over x, y, core).
Axes of the slice: x: 4, y: 8, z: 12, core: 2. Of those that a mesh axis runs over, the one named last changes fastest.
Arguments:
- patches: bfloat16 [2304, 6144], P('dp', 'mp'), may hold values from -6 to 6
- table: float32 [256, 6144], P(None, 'mp'), may hold values from -6 to 6
- row_anchor: int32 [2304, 2], P('dp'), may hold values from 0 to 14
- row_frac: float32 [2304, 2], P('dp'), may hold values from 0 to 1
- group_rows: int32 [12], replicated, may hold values from 8 to 192, as said below
- up_weight: bfloat16 [6144, 24576], P(None, 'mp'), may hold values from -0.078125 to 0.078125
- down_weight: bfloat16 [24576, 6144], P('mp'), may hold values from -0.0390625 to 0.0390625
- cotangent: bfloat16 [2304, 6144], P('dp', 'mp'), may hold values from -6 to 6
Outputs:
- grad_patches: float32 [2304, 6144], P('dp', 'mp')
- grad_table: float32 [256, 6144], P(None, 'mp')
The draws below stay inside these ranges and needn't reach their ends.
Inputs may be any that keep to these rules, and one draw needn't show every extreme that they name: `group_rows`: the entries sum to 768; one group holds exactly 192 tokens.
All inputs are finite; a program needn't handle non-finite values.
Results may differ from the reference program's by a relative error of at most 0.0026.
Values may be sent and summed in bfloat16 or wider, within the bound.
A program may use at most 64 MiB of HBM per device.

```python
import jax
import jax.numpy as jnp
from jax import lax

D = 6144
FF = 24576
GRID = 16
CELLS = 256
BAL = 64
CAP = 192
GROUPS = 12
TOKENS = 2304


def draw_group_rows(key, part):
    key = jax.random.fold_in(key, 7)
    share_key, order_key = jax.random.split(key)
    shares = jax.random.randint(share_key, (GROUPS - 1,), 4, 8).astype(jnp.int32)
    remaining = (GROUPS - 3) * BAL
    alloted = remaining * shares // jnp.sum(shares)
    alloted = alloted.at[0].add(remaining - jnp.sum(alloted))
    counts_all = jnp.concatenate([jnp.full((1,), 3 * BAL, jnp.int32), alloted.astype(jnp.int32)])
    order = jax.random.permutation(order_key, GROUPS)
    return counts_all[order].astype(jnp.int32)


def place_ends(array, stream_key, smallest, high):
    shape = array.shape
    index_at = [jax.random.randint(jax.random.fold_in(stream_key, axis), (), 0, shape[axis]) for axis in range(len(shape))]
    array = array.at[tuple(index_at)].set(smallest)
    longest = shape.index(max(shape))
    index_at[longest] = (index_at[longest] + 1) % shape[longest]
    return array.at[tuple(index_at)].set(high)


def steps_of(key, extent, cuts, low, top_value):
    factor_of, own = 1.0, jax.random.fold_in(key, 6)
    for dim, shards_of in cuts:
        draws = jnp.exp(jax.random.uniform(jax.random.fold_in(own, dim), (shards_of,), jnp.float32, low / len(cuts), top_value / len(cuts)))
        factor_of = factor_of * jnp.repeat(draws, extent[dim] // shards_of).reshape([-1 if axis == dim else 1 for axis in range(len(extent))])
    return factor_of


def normal_values(stream_key, dims, width, most, cuts=(), held_as=jnp.bfloat16):
    values = width * jax.random.normal(stream_key, dims, jnp.float32)
    if cuts:
        values = values * steps_of(stream_key, dims, cuts, -0.22, 0.18)
    return jnp.clip(values, -most, most).astype(held_as)


def setup_inputs(seed: int = 0) -> dict:
    keys = jax.random.split(jax.random.key(seed), 9)
    patches = normal_values(keys[0], (TOKENS, D), 1.0, 6.0, ((0, 12), (1, 64)))
    table = normal_values(keys[1], (CELLS, D), 1.0, 6.0, ((1, 64),), jnp.float32)
    row_anchor = place_ends(jax.random.randint(keys[2], (TOKENS, 2), 0, GRID - 1), jax.random.fold_in(keys[2], 1), 0, (GRID - 1) - 1).astype(jnp.int32)
    row_frac = jnp.clip(1.0 * jax.random.uniform(keys[3], (TOKENS, 2), jnp.float32) ** steps_of(keys[3], (TOKENS, 2), ((0, 12),), -0.2, 0.2), 0.0, 1.0)
    group_rows = draw_group_rows(jax.random.fold_in(keys[8], 71), 0)
    up_weight = normal_values(keys[5], (D, FF), D ** -0.5, 0.078125, ((1, 64),))
    down_weight = normal_values(keys[6], (FF, D), FF ** -0.5, 0.0390625, ((0, 64),))
    cotangent = normal_values(keys[7], (TOKENS, D), 1.0, 6.0, ((0, 12), (1, 64)))
    return {"patches": patches, "table": table, "row_anchor": row_anchor, "row_frac": row_frac, "group_rows": group_rows, "up_weight": up_weight, "down_weight": down_weight, "cotangent": cotangent}


def corners(row_anchor, row_frac):
    top = row_anchor[:, 0] * GRID + row_anchor[:, 1]
    cells = jnp.stack([top, top + 1, top + GRID, top + GRID + 1], axis=1).astype(jnp.int32)
    fy = row_frac[:, 0]
    fx = row_frac[:, 1]
    shares = jnp.stack([(1.0 - fy) * (1.0 - fx), (1.0 - fy) * fx, fy * (1.0 - fx), fy * fx], axis=1)
    return cells, shares


def gelu_slope(pre):
    normal_cdf = 0.5 * (1.0 + lax.erf(pre * 0.7071067811865476))
    density = jnp.exp(-0.5 * pre * pre) * 0.3989422804014327
    return normal_cdf + pre * density


def reference(patches, table, row_anchor, row_frac, group_rows, up_weight, down_weight, cotangent):
    positions = jnp.arange(TOKENS, dtype=jnp.int32)
    within = positions % CAP
    owner_group = positions // CAP
    live_rows = within < group_rows[owner_group]
    cells, shares = corners(row_anchor, row_frac)
    interp = jnp.zeros((TOKENS, D), jnp.float32)
    for corner in range(4):
        interp = interp + shares[:, corner:corner + 1] * table[cells[:, corner]]
    inputs = (patches.astype(jnp.float32) + interp).astype(jnp.bfloat16)
    pre = jnp.dot(inputs, up_weight, preferred_element_type=jnp.float32)
    back = lax.dot_general(cotangent, down_weight, (((1,), (1,)), ((), ())), preferred_element_type=jnp.float32)
    grad_pre = (back * gelu_slope(pre)).astype(jnp.bfloat16)
    branch = lax.dot_general(grad_pre, up_weight, (((1,), (1,)), ((), ())), preferred_element_type=jnp.float32)
    grad_patches = jnp.where(live_rows[:, None], cotangent.astype(jnp.float32) + branch, jnp.zeros((), jnp.float32))
    grad_table = jnp.zeros((CELLS, D), jnp.float32)
    for corner in range(4):
        grad_table = grad_table.at[cells[:, corner]].add(shares[:, corner:corner + 1] * grad_patches)
    return grad_patches, grad_table
```

```python
import jax
import jax.numpy as jnp
from jax import lax
from jax.experimental import pallas as pl
from jax.experimental.pallas import tpu as pltpu
from jax.sharding import PartitionSpec as P

MESH = pl.DeviceIdType.MESH
F32, BF16 = jnp.float32, jnp.bfloat16
GRID, CELLS, D, FF = 16, 256, 6144, 24576
NZ, NX, NY, NC = 12, 4, 8, 2
NMP = NX * NY * NC
CAP, BAL, TOKENS = 192, 64, 768
FEAT, HID = D // NMP, FF // NMP
PACK = CAP // NZ
HALF = FEAT // 2
BLOCK = NY * NC * FEAT
NN = (((1,), (0,)), ((), ()))
NT = (((1,), (1,)), ((), ()))
TN = (((0,), (0,)), ((), ()))


def dot(a, b, dims=NN):
    return lax.dot_general(a, b, dims, preferred_element_type=F32)


def iota(shape, dim):
    return lax.broadcasted_iota(jnp.int32, shape, dim)


def split2(v):
    high = v.astype(BF16)
    return high, (v - high.astype(F32)).astype(BF16)


def corner_weights(meta, first, rows):
    col = lambda k: meta[:, first + k : first + k + 1]
    a, b = col(0), col(1)
    p = (col(4) + col(3)) + col(2)
    q = (col(7) + col(6)) + col(5)
    cell = iota((rows, CELLS), 1)
    ca, cb = (cell >> 4).astype(F32), (cell & 15).astype(F32)
    wa = jnp.where(ca == a, 1.0 - p, jnp.where(ca == a + 1.0, p, 0.0))
    wb = jnp.where(cb == b, 1.0 - q, jnp.where(cb == b + 1.0, q, 0.0))
    return wa * wb


def gelu_slope(pre):
    cdf = 0.5 * (1.0 + lax.erf(pre * 0.7071067811865476))
    return cdf + pre * (jnp.exp(-0.5 * pre * pre) * 0.3989422804014327)


def kernel(
    rows_ref, patches_ref, cot_ref, table_ref, anchor_ref, frac_ref, up_hbm, down_hbm,
    gp_ref, gt_ref,
    up, down, msg, zin, cm, cmr, xt, term, sb, sr, xb, xr, yb, yr, gb, gr, own_ref,
    wsem, zs, zr, cs, cr, gys, gyr, gxs, gxr, gss, gsr, rss, rsr, rxs, rxr, rys, ryr, gzs, gzr,
):
    z, i = lax.axis_index("dp"), lax.axis_index("mp")
    x, y, c = i // (NY * NC), (i // NC) % NY, i % NC

    def device(zz, xx, yy, cc):
        return {"dp": zz, "mp": (xx * NY + yy) * NC + cc}

    zpeer = lambda o: lax.rem(z + o, NZ)
    xpeer = lambda o: lax.rem(x + o, NX)
    ypeer = lambda o: lax.rem(y + o, NY)
    sibling = device(z, x, y, 1 - c)
    sent = []

    def send(src, dst, ssem, rsem, dev):
        copy = pltpu.make_async_remote_copy(
            src_ref=src, dst_ref=dst, send_sem=ssem, recv_sem=rsem, device_id=dev, device_id_type=MESH
        )
        copy.start()
        sent.append(copy)
        return copy

    load_up = pltpu.make_async_copy(up_hbm, up, wsem.at[0])
    load_down = pltpu.make_async_copy(down_hbm, down, wsem.at[1])
    load_up.start()
    load_down.start()

    barrier = pltpu.get_barrier_semaphore()
    peers = [device(zpeer(o), x, y, c) for o in (6, 5, 7, 4, 8, 3, 9, 2, 10, 1, 11)]
    peers += [device(z, x, ypeer(o), c) for o in (4, 3, 5, 2, 6, 1, 7)]
    peers += [device(z, xpeer(o), y, c) for o in (2, 1, 3)] + [sibling]
    for dev in peers:
        pl.semaphore_signal(barrier, inc=1, device_id=dev, device_id_type=MESH)

    starts, count = [], jnp.int32(0)
    for g in range(NZ):
        starts.append(count)
        count = count + rows_ref[g]
    off = jnp.int32(0)
    for g in range(NZ):
        off = jnp.where(z == g, starts[g], off)
    own_rows = rows_ref[z]

    rho = iota((CAP, CAP), 0)
    turn = (rho >> 4) - lax.rem(off, NZ)
    slot = jnp.where(turn < 0, turn + NZ, turn) + NZ * (rho & (PACK - 1))
    perm = jnp.where(iota((CAP, CAP), 1) == slot, 1.0, 0.0).astype(BF16)

    a, b = anchor_ref[0:1, :].astype(F32), anchor_ref[1:2, :].astype(F32)
    parts = [a, b]
    for k in range(2):
        v = frac_ref[k : k + 1, :]
        for _ in range(3):
            part = v.astype(BF16).astype(F32)
            parts.append(part)
            v = v - part
    line = iota((128 - FEAT, CAP), 0)
    meta = jnp.zeros((128 - FEAT, CAP), F32)
    for k, part in enumerate(parts):
        meta = jnp.where(line == k, part, meta)
    meta = jnp.concatenate([jnp.zeros((FEAT, CAP), BF16), meta.astype(BF16)], axis=0)
    meta_rows = dot(perm, meta, NT)

    w_hi, w_lo = split2(corner_weights(meta_rows, FEAT, CAP))
    t_hi, t_lo = split2(table_ref[...])
    interp = dot(w_hi, t_hi, NT) + (dot(w_hi, t_lo, NT) + dot(w_lo, t_hi, NT))
    inputs = (dot(perm, patches_ref[...]) + interp).astype(BF16)
    msg[:, :, 0:128] = jnp.zeros((NZ, PACK, 128), BF16)
    msg[:, :, 0:FEAT] = inputs.reshape(NZ, PACK, FEAT)
    msg[:, :, 128:256] = meta_rows.astype(BF16).reshape(NZ, PACK, 128)
    msg[:, :, 128 : 128 + FEAT] = dot(perm, cot_ref[...]).astype(BF16).reshape(NZ, PACK, FEAT)

    pl.semaphore_wait(barrier, len(peers))

    z_order = (6, 5, 7, 4, 8, 3, 9, 2, 10, 1, 11)
    zc = [
        send(msg.at[zpeer(o)], zin.at[z], zs.at[o], zr.at[o], device(zpeer(o), x, y, c))
        for o in z_order
    ]
    zin[z] = msg[z]

    lane = iota((1, CAP), 1)
    group, j = lane >> 4, lane & (PACK - 1)
    place = jnp.zeros((1, CAP), jnp.int32)
    for g in range(NZ):
        o12, q12 = lax.rem(starts[g], NZ), lax.div(starts[g], NZ)
        turn = z - o12
        s = jnp.where(turn < 0, turn + NZ, turn) + NZ * j
        k = q12 + j + jnp.where(turn < 0, 1, 0)
        place = jnp.where(group == g, jnp.where(s < rows_ref[g], k, -1), place)
    compact = jnp.where(iota((BAL, CAP), 0) == place, 1.0, 0.0).astype(BF16)

    for copy in zc:
        copy.wait_recv()
    rows = dot(compact, zin[...].reshape(CAP, 256))
    both = jnp.concatenate([rows[:, :128], rows[:, 128:]], axis=0)
    xt[x, y, c] = both.T[:FEAT].astype(BF16)

    gy = [
        send(xt.at[x, y, c], xt.at[x, y, c], gys.at[o], gyr.at[o], device(z, x, ypeer(o), c))
        for o in (4, 3, 5, 2, 6, 1, 7)
    ]
    cm[...] = rows[:, 128:].astype(BF16)
    cmr[z] = cm[...]
    for copy in gy:
        copy.wait_recv()
    gx = {
        o: send(xt.at[x, :, c], xt.at[x, :, c], gxs.at[o], gxr.at[o], device(z, xpeer(o), y, c))
        for o in (2, 1, 3)
    }
    gs = {0: send(xt.at[x, :, c], xt.at[x, :, c], gss.at[0], gsr.at[0], sibling)}
    cz = [
        send(cm, cmr.at[z], cs.at[o], cr.at[o], device(zpeer(o), x, y, c)) for o in z_order
    ]

    load_up.wait()
    load_down.wait()

    def products(b):
        block = xt[b].reshape(BLOCK, 128)
        at = pl.multiple_of(b * BLOCK, BLOCK)
        return dot(block, up[pl.ds(at, BLOCK), :], TN), dot(down[:, pl.ds(at, BLOCK)], block)

    gs[0].wait_recv()
    pre, back = products(x)
    for o in (1, 3, 2):
        gx[o].wait_recv()
        b = xpeer(NX - o)
        gs[o] = send(xt.at[b, :, c], xt.at[b, :, c], gss.at[o], gsr.at[o], sibling)
    for o in (1, 3, 2):
        gs[o].wait_recv()
        more = products(xpeer(NX - o))
        pre, back = pre + more[0], back + more[1]

    low = iota((HID, 128), 1) < BAL
    grad = pltpu.roll(back, BAL, 1) * gelu_slope(pre.T)
    grad = jnp.where(low, grad, 0.0)
    pair = jnp.concatenate([grad, pltpu.roll(grad, BAL, 1)], axis=0).astype(BF16)

    rs = {}
    for o in (2, 1, 3, 0):
        b = xpeer(o)
        weights = up[pl.ds(pl.multiple_of(b * BLOCK, BLOCK), BLOCK), :]
        weights = weights.reshape(NY * NC, 2, HALF, HID)
        weights = jnp.concatenate([weights[:, 0], weights[:, 1]], axis=2)
        part = dot(weights.reshape(NY * NC * HALF, 2 * HID), pair)
        term[o] = part.reshape(NY, NC, HALF, 128)
        sb[o] = term[o, :, 1 - c].astype(BF16)
        rs[o] = send(sb.at[o], sr.at[o], rss.at[o], rsr.at[o], sibling)
    rx = []
    for o in (2, 1, 3):
        rs[o].wait_recv()
        xb[o] = (term[o, :, c] + sr[o].astype(F32)).astype(BF16)
        rx.append(send(xb.at[o], xr.at[o], rxs.at[o], rxr.at[o], device(z, xpeer(o), y, c)))

    for copy in cz:
        copy.wait_recv()
    held = cmr[...].reshape(TOKENS, 128)
    wt_hi, wt_lo = split2(corner_weights(held.astype(F32), FEAT, TOKENS))
    from_cot = (dot(held, wt_hi, TN) + dot(held, wt_lo, TN))[:FEAT]
    tau = iota((CAP, TOKENS), 1)
    rank = NZ * (tau & (BAL - 1)) + (tau >> 6)
    here = iota((CAP, TOKENS), 0)
    pick = jnp.where((rank - off == here) & (here < own_rows), 1.0, 0.0).astype(BF16)
    live_cot = jnp.where(iota((CAP, FEAT), 0) < own_rows, cot_ref[...].astype(F32), 0.0)

    rs[0].wait_recv()
    total = term[0, :, c] + sr[0].astype(F32)
    for copy in rx:
        copy.wait_recv()
    own_ref[...] = total + ((xr[1].astype(F32) + xr[3].astype(F32)) + xr[2].astype(F32))
    ry = []
    for o in (4, 3, 5, 2, 6, 1, 7):
        yb[o] = own_ref[ypeer(o)].astype(BF16)
        ry.append(send(yb.at[o], yr.at[o], rys.at[o], ryr.at[o], device(z, x, ypeer(o), c)))
    for copy in ry:
        copy.wait_recv()
    branch = own_ref[y]
    for o in range(1, NY):
        branch = branch + yr[o].astype(F32)
    gb[...] = branch.astype(BF16)
    gz = [
        send(gb, gr.at[z], gzs.at[o], gzr.at[o], device(zpeer(o), x, y, c)) for o in z_order
    ]
    gr[z] = gb[...]
    for copy in gz:
        copy.wait_recv()

    first = iota((HALF, 128), 1) < BAL
    tiles = []
    for e in range(0, NZ, 2):
        g0, g1 = gr[e].astype(F32), gr[e + 1].astype(F32)
        top = jnp.where(first, g0, pltpu.roll(g1, BAL, 1))
        bottom = jnp.where(first, pltpu.roll(g0, BAL, 1), g1)
        tiles.append(jnp.concatenate([top, bottom], axis=0).astype(BF16))
    grads = jnp.concatenate(tiles, axis=1)
    gp_ref[...] = live_cot + dot(pick, grads, NT)
    gt_ref[...] = from_cot + (dot(grads, wt_hi) + dot(grads, wt_lo))

    for copy in sent:
        copy.wait_send()


def shards(patches, table, row_anchor, row_frac, group_rows, up_weight, down_weight, cotangent):
    vmem = pl.BlockSpec(memory_space=pltpu.VMEM)
    hbm = pl.BlockSpec(memory_space=pl.ANY)
    sems = lambda n: pltpu.SemaphoreType.DMA((n,))
    grad_patches, grad_table = pl.pallas_call(
        kernel,
        name="branch_grad",
        out_shape=(
            jax.ShapeDtypeStruct((CAP, FEAT), F32),
            jax.ShapeDtypeStruct((FEAT, CELLS), F32),
        ),
        in_specs=[pl.BlockSpec(memory_space=pltpu.SMEM)] + [vmem] * 5 + [hbm] * 2,
        out_specs=(vmem, vmem),
        scratch_shapes=[
            pltpu.VMEM((D, HID), BF16),
            pltpu.VMEM((HID, D), BF16),
            pltpu.VMEM((NZ, PACK, 256), BF16),
            pltpu.VMEM((NZ, PACK, 256), BF16),
            pltpu.VMEM((BAL, 128), BF16),
            pltpu.VMEM((NZ, BAL, 128), BF16),
            pltpu.VMEM((NX, NY, NC, FEAT, 128), BF16),
            pltpu.VMEM((NX, NY, NC, HALF, 128), F32),
            pltpu.VMEM((NX, NY, HALF, 128), BF16),
            pltpu.VMEM((NX, NY, HALF, 128), BF16),
            pltpu.VMEM((NX, NY, HALF, 128), BF16),
            pltpu.VMEM((NX, NY, HALF, 128), BF16),
            pltpu.VMEM((NY, HALF, 128), BF16),
            pltpu.VMEM((NY, HALF, 128), BF16),
            pltpu.VMEM((HALF, 128), BF16),
            pltpu.VMEM((NZ, HALF, 128), BF16),
            pltpu.VMEM((NY, HALF, 128), F32),
            sems(2),
            sems(NZ), sems(NZ), sems(NZ), sems(NZ),
            sems(NY), sems(NY), sems(NX), sems(NX),
            sems(NX), sems(NX), sems(NX), sems(NX),
            sems(NX), sems(NX), sems(NY), sems(NY),
            sems(NZ), sems(NZ),
        ],
        compiler_params=pltpu.CompilerParams(
            collective_id=0, has_side_effects=True, vmem_limit_bytes=48 * 2**20
        ),
    )(
        group_rows, patches, cotangent, table.T, row_anchor.T, row_frac.T, up_weight, down_weight
    )
    return grad_patches, grad_table.T


def solution(mesh):
    in_specs = (
        P("dp", "mp"),
        P(None, "mp"),
        P("dp", None),
        P("dp", None),
        P(),
        P(None, "mp"),
        P("mp", None),
        P("dp", "mp"),
    )
    out_specs = (P("dp", "mp"), P(None, "mp"))
    return jax.shard_map(shards, mesh=mesh, in_specs=in_specs, out_specs=out_specs, check_vma=False)
```

```python
import jax
import jax.numpy as jnp
from jax import lax
from jax.experimental import pallas as pl
from jax.experimental.pallas import tpu as pltpu
from jax.sharding import PartitionSpec as P

MESH = pl.DeviceIdType.MESH
F32, BF16 = jnp.float32, jnp.bfloat16
GRID, CELLS, D, FF = 16, 256, 6144, 24576
NZ, NX, NY, NC = 12, 4, 8, 2
NMP = NX * NY * NC
CAP, BAL, TOKENS = 192, 64, 768
FEAT, HID = D // NMP, FF // NMP
PACK = CAP // NZ
HALF = FEAT // 2
BLOCK = NX * 2 * NC * FEAT
Y_ORDER = (1, 7, 6, 3, 2, 5, 4)
NN = (((1,), (0,)), ((), ()))
NT = (((1,), (1,)), ((), ()))
TN = (((0,), (0,)), ((), ()))


def dot(a, b, dims=NN):
    return lax.dot_general(a, b, dims, preferred_element_type=F32)


def iota(shape, dim):
    return lax.broadcasted_iota(jnp.int32, shape, dim)


def split2(v):
    high = v.astype(BF16)
    return high, (v - high.astype(F32)).astype(BF16)


def corner_weights(meta, first, rows):
    col = lambda k: meta[:, first + k : first + k + 1]
    a, b = col(0), col(1)
    p = (col(4) + col(3)) + col(2)
    q = (col(7) + col(6)) + col(5)
    cell = iota((rows, CELLS), 1)
    ca, cb = (cell >> 4).astype(F32), (cell & 15).astype(F32)
    wa = jnp.where(ca == a, 1.0 - p, jnp.where(ca == a + 1.0, p, 0.0))
    wb = jnp.where(cb == b, 1.0 - q, jnp.where(cb == b + 1.0, q, 0.0))
    return wa * wb


def gelu_slope(pre):
    cdf = 0.5 * (1.0 + lax.erf(pre * 0.7071067811865476))
    return cdf + pre * (jnp.exp(-0.5 * pre * pre) * 0.3989422804014327)


def kernel(
    rows_hbm, patches_hbm, cot_hbm, table_hbm, anchor_hbm, frac_hbm, up_hbm, down_hbm,
    gp_ref, gt_ref,
    rows_ref, patches_ref, cot_ref, table_ref, anchor_ref, frac_ref, up, down, msg, zin, cm, cmr, xt, up_sib, mine, theirs, xb, xr, yb, yr, gb, gr, own_ref,
    wsem, zs, zr, cs, cr, gys, gyr, gxs, gxr, gss, gsr, uss, usr, ggs, ggr, rxs, rxr, rys, ryr, gzs, gzr,
):
    z, i = lax.axis_index("dp"), lax.axis_index("mp")
    x, y, c = i // (NY * NC), (i // NC) % NY, i % NC

    def device(zz, xx, yy, cc):
        return {"dp": zz, "mp": (xx * NY + yy) * NC + cc}

    zpeer = lambda o: lax.rem(z + o, NZ)
    xpeer = lambda o: lax.rem(x + o, NX)
    flip = lambda bit, m: lax.rem(lax.rem(y // bit, 2) + (m // bit) % 2, 2) * bit
    ypeer = lambda m: flip(4, m) + flip(2, m) + flip(1, m)
    sibling = device(z, x, y, 1 - c)
    sent = []

    def send(src, dst, ssem, rsem, dev):
        copy = pltpu.make_async_remote_copy(
            src_ref=src, dst_ref=dst, send_sem=ssem, recv_sem=rsem, device_id=dev, device_id_type=MESH
        )
        copy.start()
        sent.append(copy)
        return copy

    barrier = pltpu.get_barrier_semaphore()
    peers = [device(zpeer(o), x, y, c) for o in (6, 5, 7, 4, 8, 3, 9, 2, 10, 1, 11)]
    peers += [device(z, x, ypeer(m), c) for m in Y_ORDER]
    peers += [device(z, xpeer(o), y, c) for o in (2, 1, 3)] + [sibling]
    for dev in peers:
        pl.semaphore_signal(barrier, inc=1, device_id=dev, device_id_type=MESH)

    loads = [
        pltpu.make_async_copy(src, dst, wsem.at[k])
        for k, (src, dst) in enumerate((
            (rows_hbm, rows_ref), (anchor_hbm, anchor_ref), (frac_hbm, frac_ref), (patches_hbm, patches_ref),
            (table_hbm, table_ref), (cot_hbm, cot_ref), (up_hbm, up), (down_hbm, down),
        ))
    ]
    for load in loads:
        load.start()
    for load in loads[:6]:
        load.wait()

    starts, count = [], jnp.int32(0)
    for g in range(NZ):
        starts.append(count)
        count = count + rows_ref[g]
    off = jnp.int32(0)
    for g in range(NZ):
        off = jnp.where(z == g, starts[g], off)
    own_rows = rows_ref[z]

    rho = iota((CAP, CAP), 0)
    turn = (rho >> 4) - lax.rem(off, NZ)
    slot = jnp.where(turn < 0, turn + NZ, turn) + NZ * (rho & (PACK - 1))
    perm = jnp.where(iota((CAP, CAP), 1) == slot, 1.0, 0.0).astype(BF16)

    a, b = anchor_ref[0:1, :].astype(F32), anchor_ref[1:2, :].astype(F32)
    parts = [a, b]
    for k in range(2):
        v = frac_ref[k : k + 1, :]
        for _ in range(3):
            part = v.astype(BF16).astype(F32)
            parts.append(part)
            v = v - part
    line = iota((128 - FEAT, CAP), 0)
    meta = jnp.zeros((128 - FEAT, CAP), F32)
    for k, part in enumerate(parts):
        meta = jnp.where(line == k, part, meta)
    meta = jnp.concatenate([jnp.zeros((FEAT, CAP), BF16), meta.astype(BF16)], axis=0)
    meta_rows = dot(perm, meta, NT)

    w_hi, w_lo = split2(corner_weights(meta_rows, FEAT, CAP))
    t_hi, t_lo = split2(table_ref[...])
    interp = dot(w_hi, t_hi, NT) + (dot(w_hi, t_lo, NT) + dot(w_lo, t_hi, NT))
    inputs = (dot(perm, patches_ref[...]) + interp).astype(BF16)
    msg[:, :, 0:128] = jnp.zeros((NZ, PACK, 128), BF16)
    msg[:, :, 0:FEAT] = inputs.reshape(NZ, PACK, FEAT)
    msg[:, :, 128:256] = meta_rows.astype(BF16).reshape(NZ, PACK, 128)
    msg[:, :, 128 : 128 + FEAT] = dot(perm, cot_ref[...]).astype(BF16).reshape(NZ, PACK, FEAT)

    pl.semaphore_wait(barrier, len(peers))

    z_order = (6, 5, 7, 4, 8, 3, 9, 2, 10, 1, 11)
    zc = [
        send(msg.at[zpeer(o)], zin.at[z], zs.at[o], zr.at[o], device(zpeer(o), x, y, c))
        for o in z_order
    ]
    zin[z] = msg[z]
    us = send(up_hbm.at[:, :, 1 - c], up_sib, uss.at[0], usr.at[0], sibling)

    lane = iota((1, CAP), 1)
    group, j = lane >> 4, lane & (PACK - 1)
    place = jnp.zeros((1, CAP), jnp.int32)
    for g in range(NZ):
        o12, q12 = lax.rem(starts[g], NZ), lax.div(starts[g], NZ)
        turn = z - o12
        s = jnp.where(turn < 0, turn + NZ, turn) + NZ * j
        k = q12 + j + jnp.where(turn < 0, 1, 0)
        place = jnp.where(group == g, jnp.where(s < rows_ref[g], k, -1), place)
    compact = jnp.where(iota((BAL, CAP), 0) == place, 1.0, 0.0).astype(BF16)

    for copy in zc:
        copy.wait_recv()
    rows = dot(compact, zin[...].reshape(CAP, 256))
    both = jnp.concatenate([rows[:, :128], rows[:, 128:]], axis=0)
    xt[x, y, c] = both.T[:FEAT].astype(BF16)

    def chunk(m):
        return xt.at[x, ypeer(m), c]

    def to_x(m):
        return [
            send(chunk(m), chunk(m), gxs.at[o, m], gxr.at[o, m], device(z, xpeer(o), y, c))
            for o in (2, 1, 3)
        ]

    def to_sibling(m):
        line = xt.at[:, ypeer(m), c]
        return send(line, line, gss.at[m], gsr.at[m], sibling)

    gy = {
        m: send(chunk(0), chunk(0), gys.at[m], gyr.at[m], device(z, x, ypeer(m), c))
        for m in Y_ORDER
    }
    gx = {0: to_x(0)}
    cm[...] = rows[:, 128:].astype(BF16)
    cmr[z] = cm[...]
    cz = [
        send(cm, cmr.at[z], cs.at[o], cr.at[o], device(zpeer(o), x, y, c)) for o in z_order
    ]
    for m in Y_ORDER:
        gy[m].wait_recv()
        gx[m] = to_x(m)
    for load in loads[6:]:
        load.wait()

    def products(m):
        pair = ypeer(m) // 2
        block = xt[:, pl.ds(2 * pair, 2)].reshape(BLOCK, 128)
        weights = up[:, pl.ds(2 * pair, 2)].reshape(BLOCK, HID)
        width = BLOCK // NX
        columns = [
            down[:, pl.ds(pl.multiple_of(xx * (D // NX) + pair * width, 128), width)]
            for xx in range(NX)
        ]
        return dot(block, weights, TN), dot(jnp.concatenate(columns, axis=1), block)

    gs, pre, back = {}, None, None

    def add_products(m):
        nonlocal pre, back
        gs[m].wait_recv()
        gs[m + 1].wait_recv()
        more = products(m)
        pre, back = more if pre is None else (pre + more[0], back + more[1])

    done = []
    for m in (0,) + Y_ORDER:
        for copy in gx[m]:
            copy.wait_recv()
        gs[m] = to_sibling(m)
        done.append(m)
        if len(done) % 2 == 1 and len(done) > 1:
            add_products(min(done[-3:-1]))
    add_products(min(done[-2:]))

    low = iota((HID, 128), 1) < BAL
    grad = pltpu.roll(back, BAL, 1) * gelu_slope(pre.T)
    grad = jnp.where(low, grad, 0.0)
    mine[...] = grad.astype(BF16)
    gg = send(mine, theirs, ggs.at[0], ggr.at[0], sibling)
    pair = jnp.concatenate([grad, pltpu.roll(grad, BAL, 1)], axis=0).astype(BF16)

    def terms(weights, grads):
        weights = jnp.concatenate([weights[:, 0], weights[:, 1]], axis=2)
        return dot(weights.reshape(NY * HALF, 2 * HID), grads).reshape(NY, HALF, 128)

    own_part = {o: terms(up[xpeer(o), :, c], pair) for o in (2, 1, 3, 0)}
    us.wait_recv()
    gg.wait_recv()
    grad = theirs[...].astype(F32)
    pair = jnp.concatenate([grad, pltpu.roll(grad, BAL, 1)], axis=0).astype(BF16)
    rx = []
    for o in (2, 1, 3):
        xb[o] = (own_part[o] + terms(up_sib[xpeer(o)], pair)).astype(BF16)
        rx.append(send(xb.at[o], xr.at[o], rxs.at[o], rxr.at[o], device(z, xpeer(o), y, c)))
    total = own_part[0] + terms(up_sib[x], pair)

    for copy in cz:
        copy.wait_recv()
    held = cmr[...].reshape(TOKENS, 128)
    wt_hi, wt_lo = split2(corner_weights(held.astype(F32), FEAT, TOKENS))
    from_cot = (dot(held, wt_hi, TN) + dot(held, wt_lo, TN))[:FEAT]
    tau = iota((CAP, TOKENS), 1)
    rank = NZ * (tau & (BAL - 1)) + (tau >> 6)
    here = iota((CAP, TOKENS), 0)
    pick = jnp.where((rank - off == here) & (here < own_rows), 1.0, 0.0).astype(BF16)
    live_cot = jnp.where(iota((CAP, FEAT), 0) < own_rows, cot_ref[...].astype(F32), 0.0)

    for copy in rx:
        copy.wait_recv()
    own_ref[...] = total + ((xr[1].astype(F32) + xr[3].astype(F32)) + xr[2].astype(F32))
    ry = []
    for m in reversed(Y_ORDER):
        yb[m] = own_ref[ypeer(m)].astype(BF16)
        ry.append(send(yb.at[m], yr.at[m], rys.at[m], ryr.at[m], device(z, x, ypeer(m), c)))
    for copy in ry:
        copy.wait_recv()
    branch = own_ref[y]
    for o in range(1, NY):
        branch = branch + yr[o].astype(F32)
    gb[...] = branch.astype(BF16)
    gz = [
        send(gb, gr.at[z], gzs.at[o], gzr.at[o], device(zpeer(o), x, y, c)) for o in z_order
    ]
    gr[z] = gb[...]
    for copy in gz:
        copy.wait_recv()

    first = iota((HALF, 128), 1) < BAL
    tiles = []
    for e in range(0, NZ, 2):
        g0, g1 = gr[e].astype(F32), gr[e + 1].astype(F32)
        top = jnp.where(first, g0, pltpu.roll(g1, BAL, 1))
        bottom = jnp.where(first, pltpu.roll(g0, BAL, 1), g1)
        tiles.append(jnp.concatenate([top, bottom], axis=0).astype(BF16))
    grads = jnp.concatenate(tiles, axis=1)
    gp_ref[...] = live_cot + dot(pick, grads, NT)
    gt_ref[...] = from_cot + (dot(grads, wt_hi) + dot(grads, wt_lo))

    for copy in sent:
        copy.wait_send()


def copy_out(a_ref, b_ref, a_out, b_out):
    a_out[...] = a_ref[...]
    b_out[...] = b_ref[...]


def shards(patches, table, row_anchor, row_frac, group_rows, up_weight, down_weight, cotangent):
    vmem = pl.BlockSpec(memory_space=pltpu.VMEM)
    hbm = pl.BlockSpec(memory_space=pltpu.HBM)
    sems = lambda *n: pltpu.SemaphoreType.DMA(n)
    grad_patches, grad_table = pl.pallas_call(
        kernel,
        name="branch_grad",
        out_shape=(
            jax.ShapeDtypeStruct((CAP, FEAT), F32),
            jax.ShapeDtypeStruct((FEAT, CELLS), F32),
        ),
        in_specs=[hbm] * 8,
        out_specs=(vmem, vmem),
        scratch_shapes=[
            pltpu.SMEM((NZ,), jnp.int32),
            pltpu.VMEM((CAP, FEAT), BF16),
            pltpu.VMEM((CAP, FEAT), BF16),
            pltpu.VMEM((FEAT, CELLS), F32),
            pltpu.VMEM((2, CAP), jnp.int32),
            pltpu.VMEM((2, CAP), F32),
            pltpu.VMEM((NX, NY, NC, 2, HALF, HID), BF16),
            pltpu.VMEM((HID, D), BF16),
            pltpu.VMEM((NZ, PACK, 256), BF16),
            pltpu.VMEM((NZ, PACK, 256), BF16),
            pltpu.VMEM((BAL, 128), BF16),
            pltpu.VMEM((NZ, BAL, 128), BF16),
            pltpu.VMEM((NX, NY, NC, FEAT, 128), BF16),
            pltpu.VMEM((NX, NY, 2, HALF, HID), BF16),
            pltpu.VMEM((HID, 128), BF16),
            pltpu.VMEM((HID, 128), BF16),
            pltpu.VMEM((NX, NY, HALF, 128), BF16),
            pltpu.VMEM((NX, NY, HALF, 128), BF16),
            pltpu.VMEM((NY, HALF, 128), BF16),
            pltpu.VMEM((NY, HALF, 128), BF16),
            pltpu.VMEM((HALF, 128), BF16),
            pltpu.VMEM((NZ, HALF, 128), BF16),
            pltpu.VMEM((NY, HALF, 128), F32),
            sems(8),
            sems(NZ), sems(NZ), sems(NZ), sems(NZ),
            sems(NY), sems(NY), sems(NX, NY), sems(NX, NY), sems(NY), sems(NY), sems(1), sems(1), sems(1), sems(1),
            sems(NX), sems(NX), sems(NY), sems(NY),
            sems(NZ), sems(NZ),
        ],
        compiler_params=pltpu.CompilerParams(
            collective_id=0, has_side_effects=True, vmem_limit_bytes=60 * 2**20
        ),
    )(
        group_rows, patches, cotangent, table.T, row_anchor.T, row_frac.T,
        up_weight.reshape(NX, NY, NC, 2, HALF, HID), down_weight,
    )
    grad_patches, grad_table = pl.pallas_call(
        copy_out,
        name="copy_out",
        out_shape=(
            jax.ShapeDtypeStruct((CAP, FEAT), F32),
            jax.ShapeDtypeStruct((FEAT, CELLS), F32),
        ),
        in_specs=[vmem] * 2,
        out_specs=(vmem, vmem),
    )(grad_patches, grad_table)
    return grad_patches, grad_table.T


def solution(mesh):
    in_specs = (
        P("dp", "mp"),
        P(None, "mp"),
        P("dp", None),
        P("dp", None),
        P(),
        P(None, "mp"),
        P("mp", None),
        P("dp", "mp"),
    )
    out_specs = (P("dp", "mp"), P(None, "mp"))
    return jax.shard_map(shards, mesh=mesh, in_specs=in_specs, out_specs=out_specs, check_vma=False)
```

```python
import jax
import jax.numpy as jnp
from jax import lax
from jax.experimental import pallas as pl
from jax.experimental.pallas import tpu as pltpu
from jax.sharding import PartitionSpec as P

MESH = pl.DeviceIdType.MESH
F32, BF16 = jnp.float32, jnp.bfloat16
GRID, CELLS, D, FF = 16, 256, 6144, 24576
NZ, NX, NY, NC = 12, 4, 8, 2
NMP = NX * NY * NC
CAP, BAL, TOKENS = 192, 64, 768
FEAT, HID = D // NMP, FF // NMP
PACK = CAP // NZ
HALF = FEAT // 2
BLOCK = NX * 2 * NC * FEAT
Y_ORDER = (1, 7, 2, 6, 3, 5, 4)
STREAMS = ((0, 16), (16, 32))
NN = (((1,), (0,)), ((), ()))
NT = (((1,), (1,)), ((), ()))
TN = (((0,), (0,)), ((), ()))


def dot(a, b, dims=NN):
    return lax.dot_general(a, b, dims, preferred_element_type=F32)


def iota(shape, dim):
    return lax.broadcasted_iota(jnp.int32, shape, dim)


def split2(v):
    high = v.astype(BF16)
    return high, (v - high.astype(F32)).astype(BF16)


def corner_weights(meta, first, rows):
    col = lambda k: meta[:, first + k : first + k + 1]
    a, b = col(0), col(1)
    p = (col(4) + col(3)) + col(2)
    q = (col(7) + col(6)) + col(5)
    cell = iota((rows, CELLS), 1)
    ca, cb = (cell >> 4).astype(F32), (cell & 15).astype(F32)
    wa = jnp.where(ca == a, 1.0 - p, jnp.where(ca == a + 1.0, p, 0.0))
    wb = jnp.where(cb == b, 1.0 - q, jnp.where(cb == b + 1.0, q, 0.0))
    return wa * wb


def gelu_slope(pre):
    cdf = 0.5 * (1.0 + lax.erf(pre * 0.7071067811865476))
    return cdf + pre * (jnp.exp(-0.5 * pre * pre) * 0.3989422804014327)


def kernel(
    rows_hbm, patches_hbm, cot_hbm, table_hbm, anchor_hbm, frac_hbm, up_hbm, down_hbm,
    gp_ref, gt_ref,
    rows_ref, patches_ref, cot_ref, table_ref, anchor_ref, frac_ref, up, down, msg, zin, cm, cmr, xt, up_sib, mine, theirs, xb, xr, yb, yr, gb, gr, own_ref,
    wsem, zs, zr, cs, cr, gys, gyr, gxs, gxr, gss, gsr, uss, usr, ggs, ggr, rxs, rxr, rys, ryr, gzs, gzr,
):
    z, i = lax.axis_index("dp"), lax.axis_index("mp")
    x, y, c = i // (NY * NC), (i // NC) % NY, i % NC

    def device(zz, xx, yy, cc):
        return {"dp": zz, "mp": (xx * NY + yy) * NC + cc}

    zpeer = lambda o: lax.rem(z + o, NZ)
    xpeer = lambda o: lax.rem(x + o, NX)
    ypeer = lambda o: lax.rem(y + o, NY)
    sibling = device(z, x, y, 1 - c)
    sent = []

    def send(src, dst, ssem, rsem, dev):
        copy = pltpu.make_async_remote_copy(
            src_ref=src, dst_ref=dst, send_sem=ssem, recv_sem=rsem, device_id=dev, device_id_type=MESH
        )
        copy.start()
        sent.append(copy)
        return copy

    barrier = pltpu.get_barrier_semaphore()
    peers = [device(zpeer(o), x, y, c) for o in (6, 5, 7, 4, 8, 3, 9, 2, 10, 1, 11)]
    peers += [device(z, x, ypeer(m), c) for m in Y_ORDER]
    peers += [device(z, xpeer(o), y, c) for o in (2, 1, 3)] + [sibling]
    for dev in peers:
        pl.semaphore_signal(barrier, inc=1, device_id=dev, device_id_type=MESH)

    loads = [
        pltpu.make_async_copy(src, dst, wsem.at[k])
        for k, (src, dst) in enumerate((
            (rows_hbm, rows_ref), (anchor_hbm, anchor_ref), (frac_hbm, frac_ref), (patches_hbm, patches_ref),
            (table_hbm, table_ref), (cot_hbm, cot_ref), (up_hbm, up), (down_hbm, down),
        ))
    ]
    for load in loads:
        load.start()
    for load in loads[:6]:
        load.wait()

    starts, count = [], jnp.int32(0)
    for g in range(NZ):
        starts.append(count)
        count = count + rows_ref[g]
    off = jnp.int32(0)
    for g in range(NZ):
        off = jnp.where(z == g, starts[g], off)
    own_rows = rows_ref[z]

    rho = iota((CAP, CAP), 0)
    turn = (rho >> 4) - lax.rem(off, NZ)
    slot = jnp.where(turn < 0, turn + NZ, turn) + NZ * (rho & (PACK - 1))
    perm = jnp.where(iota((CAP, CAP), 1) == slot, 1.0, 0.0).astype(BF16)

    a, b = anchor_ref[0:1, :].astype(F32), anchor_ref[1:2, :].astype(F32)
    parts = [a, b]
    for k in range(2):
        v = frac_ref[k : k + 1, :]
        for _ in range(3):
            part = v.astype(BF16).astype(F32)
            parts.append(part)
            v = v - part
    line = iota((128 - FEAT, CAP), 0)
    meta = jnp.zeros((128 - FEAT, CAP), F32)
    for k, part in enumerate(parts):
        meta = jnp.where(line == k, part, meta)
    meta = jnp.concatenate([jnp.zeros((FEAT, CAP), BF16), meta.astype(BF16)], axis=0)
    meta_rows = dot(perm, meta, NT)

    w_hi, w_lo = split2(corner_weights(meta_rows, FEAT, CAP))
    t_hi, t_lo = split2(table_ref[...])
    interp = dot(w_hi, t_hi, NT) + (dot(w_hi, t_lo, NT) + dot(w_lo, t_hi, NT))
    inputs = (dot(perm, patches_ref[...]) + interp).astype(BF16)
    msg[:, :, 0:128] = jnp.zeros((NZ, PACK, 128), BF16)
    msg[:, :, 0:FEAT] = inputs.reshape(NZ, PACK, FEAT)
    msg[:, :, 128:256] = meta_rows.astype(BF16).reshape(NZ, PACK, 128)
    msg[:, :, 128 : 128 + FEAT] = dot(perm, cot_ref[...]).astype(BF16).reshape(NZ, PACK, FEAT)

    pl.semaphore_wait(barrier, len(peers))

    z_order = (6, 5, 7, 4, 8, 3, 9, 2, 10, 1, 11)
    zc = [
        send(msg.at[zpeer(o)], zin.at[z], zs.at[o], zr.at[o], device(zpeer(o), x, y, c))
        for o in z_order
    ]
    zin[z] = msg[z]
    us = send(up_hbm.at[:, :, 1 - c], up_sib, uss.at[0], usr.at[0], sibling)

    lane = iota((1, CAP), 1)
    group, j = lane >> 4, lane & (PACK - 1)
    place = jnp.zeros((1, CAP), jnp.int32)
    for g in range(NZ):
        o12, q12 = lax.rem(starts[g], NZ), lax.div(starts[g], NZ)
        turn = z - o12
        s = jnp.where(turn < 0, turn + NZ, turn) + NZ * j
        k = q12 + j + jnp.where(turn < 0, 1, 0)
        place = jnp.where(group == g, jnp.where(s < rows_ref[g], k, -1), place)
    compact = jnp.where(iota((BAL, CAP), 0) == place, 1.0, 0.0).astype(BF16)

    for copy in zc:
        copy.wait_recv()
    rows = dot(compact, zin[...].reshape(CAP, 256))
    both = jnp.concatenate([rows[:, :128], rows[:, 128:]], axis=0)
    xt[x, y, c] = both.T[:FEAT].astype(BF16)

    def chunk(m):
        return xt.at[x, ypeer(NY - m), c]

    def to_x(m):
        return [
            send(chunk(m), chunk(m), gxs.at[o, m], gxr.at[o, m], device(z, xpeer(o), y, c))
            for o in (2, 1, 3)
        ]

    def to_sibling(m):
        line = xt.at[:, ypeer(NY - m), c]
        return send(line, line, gss.at[m], gsr.at[m], sibling)

    gy = {
        m: send(chunk(0), chunk(0), gys.at[m], gyr.at[m], device(z, x, ypeer(m), c))
        for m in Y_ORDER
    }
    gx = {0: to_x(0)}
    cm[...] = rows[:, 128:].astype(BF16)
    cmr[z] = cm[...]
    cz = [
        send(cm, cmr.at[z], cs.at[o], cr.at[o], device(zpeer(o), x, y, c)) for o in z_order
    ]
    for m in Y_ORDER:
        gy[m].wait_recv()
        gx[m] = to_x(m)
    for load in loads[6:]:
        load.wait()

    def products(pair):
        block = xt[:, pl.ds(2 * pair, 2)].reshape(BLOCK, 128)
        weights = up[:, pl.ds(2 * pair, 2)].reshape(BLOCK, HID)
        width = BLOCK // NX
        columns = [
            down[:, pl.ds(pl.multiple_of(xx * (D // NX) + pair * width, 128), width)]
            for xx in range(NX)
        ]
        return dot(block, weights, TN), dot(jnp.concatenate(columns, axis=1), block)

    half, odd = y // 2, lax.rem(y, 2)
    turns = (0, 3 - 2 * odd, 1 + 2 * odd, 2)
    gs, pre, back, whole = {}, None, None, []
    arrivals = (0,) + Y_ORDER
    for n, m in enumerate(arrivals):
        for copy in gx[m]:
            copy.wait_recv()
        gs[m] = to_sibling(m)
        for t in {3: (0,), 5: (1,), 7: (2, 3)}.get(n, ()):
            for k in arrivals[: (3, 5, 7, 8)[t]]:
                if k not in whole:
                    gs[k].wait_recv()
                    whole.append(k)
            more = products(lax.rem(half + turns[t], NY // 2))
            pre, back = more if pre is None else (pre + more[0], back + more[1])

    low = iota((HID, 128), 1) < BAL
    grad = pltpu.roll(back, BAL, 1) * gelu_slope(pre.T)
    grad = jnp.where(low, grad, 0.0)
    mine[...] = grad.astype(BF16)
    gg = send(mine, theirs, ggs.at[0], ggr.at[0], sibling)
    pair = jnp.concatenate([grad, pltpu.roll(grad, BAL, 1)], axis=0).astype(BF16)

    def terms(weights, grads, first, n):
        weights = weights[:, :, first : first + n]
        weights = jnp.concatenate([weights[:, 0], weights[:, 1]], axis=2)
        return dot(weights.reshape(NY * n, 2 * HID), grads).reshape(NY, n, 128)

    own_part = {
        (h, o): terms(up[xpeer(o), :, c], pair, *rows)
        for h, rows in enumerate(STREAMS)
        for o in (2, 1, 3, 0)
    }
    us.wait_recv()
    gg.wait_recv()
    grad = theirs[...].astype(F32)
    pair = jnp.concatenate([grad, pltpu.roll(grad, BAL, 1)], axis=0).astype(BF16)
    rx = {}
    for h, (first, n) in enumerate(STREAMS):
        at = pl.ds(first, n)
        for o in (2, 1, 3):
            part = own_part[h, o] + terms(up_sib[xpeer(o)], pair, first, n)
            xb[o, :, at] = part.astype(BF16)
            rx[h, o] = send(
                xb.at[o, :, at], xr.at[o, :, at], rxs.at[h, o], rxr.at[h, o], device(z, xpeer(o), y, c)
            )
    for h, (first, n) in enumerate(STREAMS):
        own_ref[:, pl.ds(first, n)] = own_part[h, 0] + terms(up_sib[x], pair, first, n)

    for copy in cz:
        copy.wait_recv()
    held = cmr[...].reshape(TOKENS, 128)
    wt_hi, wt_lo = split2(corner_weights(held.astype(F32), FEAT, TOKENS))
    from_cot = (dot(held, wt_hi, TN) + dot(held, wt_lo, TN))[:FEAT]

    ry = {}
    for h, (first, n) in enumerate(STREAMS):
        at = pl.ds(first, n)
        for o in (2, 1, 3):
            rx[h, o].wait_recv()
        total = xr[1, :, at].astype(F32) + xr[3, :, at].astype(F32)
        own_ref[:, at] = own_ref[:, at] + (total + xr[2, :, at].astype(F32))
        for m in reversed(Y_ORDER):
            yb[m, at] = own_ref[ypeer(m), at].astype(BF16)
            ry[h, m] = send(
                yb.at[m, at], yr.at[m, at], rys.at[h, m], ryr.at[h, m], device(z, x, ypeer(m), c)
            )
    tau = iota((CAP, TOKENS), 1)
    rank = NZ * (tau & (BAL - 1)) + (tau >> 6)
    here = iota((CAP, TOKENS), 0)
    pick = jnp.where((rank - off == here) & (here < own_rows), 1.0, 0.0).astype(BF16)
    live_cot = jnp.where(iota((CAP, FEAT), 0) < own_rows, cot_ref[...].astype(F32), 0.0)
    gz = []
    for h, (first, n) in enumerate(STREAMS):
        at = pl.ds(first, n)
        for m in Y_ORDER:
            ry[h, m].wait_recv()
        branch = own_ref[y, at]
        for m in range(1, NY):
            branch = branch + yr[m, at].astype(F32)
        gb[at] = branch.astype(BF16)
        gz += [
            send(gb.at[at], gr.at[z, at], gzs.at[h, o], gzr.at[h, o], device(zpeer(o), x, y, c))
            for o in z_order
        ]
    gr[z] = gb[...]
    for copy in gz:
        copy.wait_recv()

    first = iota((HALF, 128), 1) < BAL
    tiles = []
    for e in range(0, NZ, 2):
        g0, g1 = gr[e].astype(F32), gr[e + 1].astype(F32)
        top = jnp.where(first, g0, pltpu.roll(g1, BAL, 1))
        bottom = jnp.where(first, pltpu.roll(g0, BAL, 1), g1)
        tiles.append(jnp.concatenate([top, bottom], axis=0).astype(BF16))
    grads = jnp.concatenate(tiles, axis=1)
    gp_ref[...] = live_cot + dot(pick, grads, NT)
    gt_ref[...] = from_cot + (dot(grads, wt_hi) + dot(grads, wt_lo))

    for copy in sent:
        copy.wait_send()


def copy_out(a_ref, b_ref, a_out, b_out):
    a_out[...] = a_ref[...]
    b_out[...] = b_ref[...]


def shards(patches, table, row_anchor, row_frac, group_rows, up_weight, down_weight, cotangent):
    vmem = pl.BlockSpec(memory_space=pltpu.VMEM)
    hbm = pl.BlockSpec(memory_space=pltpu.HBM)
    sems = lambda *n: pltpu.SemaphoreType.DMA(n)
    grad_patches, grad_table = pl.pallas_call(
        kernel,
        name="branch_grad",
        out_shape=(
            jax.ShapeDtypeStruct((CAP, FEAT), F32),
            jax.ShapeDtypeStruct((FEAT, CELLS), F32),
        ),
        in_specs=[hbm] * 8,
        out_specs=(vmem, vmem),
        scratch_shapes=[
            pltpu.SMEM((NZ,), jnp.int32),
            pltpu.VMEM((CAP, FEAT), BF16),
            pltpu.VMEM((CAP, FEAT), BF16),
            pltpu.VMEM((FEAT, CELLS), F32),
            pltpu.VMEM((2, CAP), jnp.int32),
            pltpu.VMEM((2, CAP), F32),
            pltpu.VMEM((NX, NY, NC, 2, HALF, HID), BF16),
            pltpu.VMEM((HID, D), BF16),
            pltpu.VMEM((NZ, PACK, 256), BF16),
            pltpu.VMEM((NZ, PACK, 256), BF16),
            pltpu.VMEM((BAL, 128), BF16),
            pltpu.VMEM((NZ, BAL, 128), BF16),
            pltpu.VMEM((NX, NY, NC, FEAT, 128), BF16),
            pltpu.VMEM((NX, NY, 2, HALF, HID), BF16),
            pltpu.VMEM((HID, 128), BF16),
            pltpu.VMEM((HID, 128), BF16),
            pltpu.VMEM((NX, NY, HALF, 128), BF16),
            pltpu.VMEM((NX, NY, HALF, 128), BF16),
            pltpu.VMEM((NY, HALF, 128), BF16),
            pltpu.VMEM((NY, HALF, 128), BF16),
            pltpu.VMEM((HALF, 128), BF16),
            pltpu.VMEM((NZ, HALF, 128), BF16),
            pltpu.VMEM((NY, HALF, 128), F32),
            sems(8),
            sems(NZ), sems(NZ), sems(NZ), sems(NZ),
            sems(NY), sems(NY), sems(NX, NY), sems(NX, NY), sems(NY), sems(NY), sems(1), sems(1), sems(1), sems(1),
            sems(2, NX), sems(2, NX), sems(2, NY), sems(2, NY),
            sems(2, NZ), sems(2, NZ),
        ],
        compiler_params=pltpu.CompilerParams(
            collective_id=0, has_side_effects=True, vmem_limit_bytes=60 * 2**20
        ),
    )(
        group_rows, patches, cotangent, table.T, row_anchor.T, row_frac.T,
        up_weight.reshape(NX, NY, NC, 2, HALF, HID), down_weight,
    )
    grad_patches, grad_table = pl.pallas_call(
        copy_out,
        name="copy_out",
        out_shape=(
            jax.ShapeDtypeStruct((CAP, FEAT), F32),
            jax.ShapeDtypeStruct((FEAT, CELLS), F32),
        ),
        in_specs=[vmem] * 2,
        out_specs=(vmem, vmem),
    )(grad_patches, grad_table)
    return grad_patches, grad_table.T


def solution(mesh):
    in_specs = (
        P("dp", "mp"),
        P(None, "mp"),
        P("dp", None),
        P("dp", None),
        P(),
        P(None, "mp"),
        P("mp", None),
        P("dp", "mp"),
    )
    out_specs = (P("dp", "mp"), P(None, "mp"))
    return jax.shard_map(shards, mesh=mesh, in_specs=in_specs, out_specs=out_specs, check_vma=False)
```

```python
import jax
import jax.numpy as jnp
from jax import lax
from jax.experimental import pallas as pl
from jax.experimental.pallas import tpu as pltpu
from jax.sharding import PartitionSpec as P

MESH = pl.DeviceIdType.MESH
F32, BF16 = jnp.float32, jnp.bfloat16
GRID, CELLS, D, FF = 16, 256, 6144, 24576
NZ, NX, NY, NC = 12, 4, 8, 2
NMP = NX * NY * NC
CAP, BAL, TOKENS = 192, 64, 768
FEAT, HID = D // NMP, FF // NMP
PACK = CAP // NZ
HALF = FEAT // 2
BLOCK = NX * 2 * NC * FEAT
Y_ORDER = (1, 7, 4, 3, 5, 2, 6)
Y_FAR = (4, 5, 3, 6, 2, 7, 1)
STREAMS = ((0, 16), (16, 16), (32, 16))
NN = (((1,), (0,)), ((), ()))
NT = (((1,), (1,)), ((), ()))
TN = (((0,), (0,)), ((), ()))


def dot(a, b, dims=NN):
    return lax.dot_general(a, b, dims, preferred_element_type=F32)


def iota(shape, dim):
    return lax.broadcasted_iota(jnp.int32, shape, dim)


def split2(v):
    high = v.astype(BF16)
    return high, (v - high.astype(F32)).astype(BF16)


def corner_weights(meta, first, rows):
    col = lambda k: meta[:, first + k : first + k + 1]
    a, b = col(0), col(1)
    p = (col(4) + col(3)) + col(2)
    q = (col(7) + col(6)) + col(5)
    cell = iota((rows, CELLS), 1)
    ca, cb = (cell >> 4).astype(F32), (cell & 15).astype(F32)
    wa = jnp.where(ca == a, 1.0 - p, jnp.where(ca == a + 1.0, p, 0.0))
    wb = jnp.where(cb == b, 1.0 - q, jnp.where(cb == b + 1.0, q, 0.0))
    return wa * wb


def gelu_slope(pre):
    cdf = 0.5 * (1.0 + lax.erf(pre * 0.7071067811865476))
    return cdf + pre * (jnp.exp(-0.5 * pre * pre) * 0.3989422804014327)


def kernel(
    rows_hbm, patches_hbm, cot_hbm, table_hbm, anchor_hbm, frac_hbm, up_hbm, down_hbm,
    gp_ref, gt_ref,
    rows_ref, patches_ref, cot_ref, table_ref, anchor_ref, frac_ref, up, down, msg, zin, cm, cmr, xt, up_sib, mine, theirs, xb, xr, yb, yr, gb, gr, own_ref,
    wsem, zs, zr, cs, cr, gys, gyr, gxs, gxr, gss, gsr, uss, usr, ggs, ggr, rxs, rxr, rys, ryr, gzs, gzr,
):
    z, i = lax.axis_index("dp"), lax.axis_index("mp")
    x, y, c = i // (NY * NC), (i // NC) % NY, i % NC

    def device(zz, xx, yy, cc):
        return {"dp": zz, "mp": (xx * NY + yy) * NC + cc}

    zpeer = lambda o: lax.rem(z + o, NZ)
    xpeer = lambda o: lax.rem(x + o, NX)
    ypeer = lambda o: lax.rem(y + o, NY)
    sibling = device(z, x, y, 1 - c)
    sent = []

    def send(src, dst, ssem, rsem, dev):
        copy = pltpu.make_async_remote_copy(
            src_ref=src, dst_ref=dst, send_sem=ssem, recv_sem=rsem, device_id=dev, device_id_type=MESH
        )
        copy.start()
        sent.append(copy)
        return copy

    barrier = pltpu.get_barrier_semaphore()
    peers = [device(zpeer(o), x, y, c) for o in (6, 5, 7, 4, 8, 3, 9, 2, 10, 1, 11)]
    peers += [device(z, x, ypeer(m), c) for m in Y_ORDER]
    peers += [device(z, xpeer(o), y, c) for o in (2, 1, 3)] + [sibling]
    for dev in peers:
        pl.semaphore_signal(barrier, inc=1, device_id=dev, device_id_type=MESH)

    loads = [
        pltpu.make_async_copy(src, dst, wsem.at[k])
        for k, (src, dst) in enumerate((
            (rows_hbm, rows_ref), (anchor_hbm, anchor_ref), (frac_hbm, frac_ref), (patches_hbm, patches_ref),
            (table_hbm, table_ref), (cot_hbm, cot_ref), (up_hbm, up), (down_hbm, down),
        ))
    ]
    for load in loads:
        load.start()
    for load in loads[:6]:
        load.wait()

    starts, count = [], jnp.int32(0)
    for g in range(NZ):
        starts.append(count)
        count = count + rows_ref[g]
    off = jnp.int32(0)
    for g in range(NZ):
        off = jnp.where(z == g, starts[g], off)
    own_rows = rows_ref[z]

    rho = iota((CAP, CAP), 0)
    turn = (rho >> 4) - lax.rem(off, NZ)
    slot = jnp.where(turn < 0, turn + NZ, turn) + NZ * (rho & (PACK - 1))
    perm = jnp.where(iota((CAP, CAP), 1) == slot, 1.0, 0.0).astype(BF16)

    a, b = anchor_ref[0:1, :].astype(F32), anchor_ref[1:2, :].astype(F32)
    parts = [a, b]
    for k in range(2):
        v = frac_ref[k : k + 1, :]
        for _ in range(3):
            part = v.astype(BF16).astype(F32)
            parts.append(part)
            v = v - part
    line = iota((128 - FEAT, CAP), 0)
    meta = jnp.zeros((128 - FEAT, CAP), F32)
    for k, part in enumerate(parts):
        meta = jnp.where(line == k, part, meta)
    meta = jnp.concatenate([jnp.zeros((FEAT, CAP), BF16), meta.astype(BF16)], axis=0)
    meta_rows = dot(perm, meta, NT)

    w_hi, w_lo = split2(corner_weights(meta_rows, FEAT, CAP))
    t_hi, t_lo = split2(table_ref[...])
    interp = dot(w_hi, t_hi, NT) + (dot(w_hi, t_lo, NT) + dot(w_lo, t_hi, NT))
    inputs = (dot(perm, patches_ref[...]) + interp).astype(BF16)
    msg[:, :, 0:128] = jnp.zeros((NZ, PACK, 128), BF16)
    msg[:, :, 0:FEAT] = inputs.reshape(NZ, PACK, FEAT)
    msg[:, :, 128:256] = meta_rows.astype(BF16).reshape(NZ, PACK, 128)
    msg[:, :, 128 : 128 + FEAT] = dot(perm, cot_ref[...]).astype(BF16).reshape(NZ, PACK, FEAT)

    pl.semaphore_wait(barrier, len(peers))

    z_order = (6, 5, 7, 4, 8, 3, 9, 2, 10, 1, 11)
    zc = [
        send(msg.at[zpeer(o)], zin.at[z], zs.at[o], zr.at[o], device(zpeer(o), x, y, c))
        for o in z_order
    ]
    zin[z] = msg[z]
    us = send(up_hbm.at[:, :, 1 - c], up_sib, uss.at[0], usr.at[0], sibling)

    lane = iota((1, CAP), 1)
    group, j = lane >> 4, lane & (PACK - 1)
    place = jnp.zeros((1, CAP), jnp.int32)
    for g in range(NZ):
        o12, q12 = lax.rem(starts[g], NZ), lax.div(starts[g], NZ)
        turn = z - o12
        s = jnp.where(turn < 0, turn + NZ, turn) + NZ * j
        k = q12 + j + jnp.where(turn < 0, 1, 0)
        place = jnp.where(group == g, jnp.where(s < rows_ref[g], k, -1), place)
    compact = jnp.where(iota((BAL, CAP), 0) == place, 1.0, 0.0).astype(BF16)

    for copy in zc:
        copy.wait_recv()
    rows = dot(compact, zin[...].reshape(CAP, 256))
    both = jnp.concatenate([rows[:, :128], rows[:, 128:]], axis=0)
    xt[x, y, c] = both.T[:FEAT].astype(BF16)

    def chunk(m):
        return xt.at[x, ypeer(NY - m), c]

    def to_x(m):
        return [
            send(chunk(m), chunk(m), gxs.at[o, m], gxr.at[o, m], device(z, xpeer(o), y, c))
            for o in (2, 1, 3)
        ]

    def to_sibling(m):
        line = xt.at[:, ypeer(NY - m), c]
        return send(line, line, gss.at[m], gsr.at[m], sibling)

    gy = {
        m: send(chunk(0), chunk(0), gys.at[m], gyr.at[m], device(z, x, ypeer(m), c))
        for m in Y_ORDER
    }
    gx = {0: to_x(0)}
    cm[...] = rows[:, 128:].astype(BF16)
    cmr[z] = cm[...]
    cz = [
        send(cm, cmr.at[z], cs.at[o], cr.at[o], device(zpeer(o), x, y, c)) for o in z_order
    ]
    for m in Y_ORDER:
        gy[m].wait_recv()
        gx[m] = to_x(m)
    for load in loads[6:]:
        load.wait()

    def products(pair):
        block = xt[:, pl.ds(2 * pair, 2)].reshape(BLOCK, 128)
        weights = up[:, pl.ds(2 * pair, 2)].reshape(BLOCK, HID)
        width = BLOCK // NX
        columns = [
            down[:, pl.ds(pl.multiple_of(xx * (D // NX) + pair * width, 128), width)]
            for xx in range(NX)
        ]
        return dot(block, weights, TN), dot(jnp.concatenate(columns, axis=1), block)

    half, turns = y // 2, (0, 2, 3, 1)
    gs, pre, back, whole = {}, None, None, []
    arrivals = (0,) + Y_ORDER
    for n, m in enumerate(arrivals):
        for copy in gx[m]:
            copy.wait_recv()
        gs[m] = to_sibling(m)
        for t in {3: (0,), 6: (1,), 7: (2, 3)}.get(n, ()):
            for k in arrivals[: (3, 6, 7, 8)[t]]:
                if k not in whole:
                    gs[k].wait_recv()
                    whole.append(k)
            more = products(lax.rem(half + turns[t], NY // 2))
            pre, back = more if pre is None else (pre + more[0], back + more[1])

    low = iota((HID, 128), 1) < BAL
    grad = pltpu.roll(back, BAL, 1) * gelu_slope(pre.T)
    grad = jnp.where(low, grad, 0.0)
    mine[...] = grad.astype(BF16)
    gg = send(mine, theirs, ggs.at[0], ggr.at[0], sibling)
    pair = jnp.concatenate([grad, pltpu.roll(grad, BAL, 1)], axis=0).astype(BF16)

    def terms(weights, grads, first, n):
        weights = weights[:, :, first : first + n]
        weights = jnp.concatenate([weights[:, 0], weights[:, 1]], axis=2)
        return dot(weights.reshape(NY * n, 2 * HID), grads).reshape(NY, n, 128)

    own_part = {
        (h, o): terms(up[xpeer(o), :, c], pair, *rows)
        for h, rows in enumerate(STREAMS)
        for o in (2, 1, 3, 0)
    }
    us.wait_recv()
    gg.wait_recv()
    grad = theirs[...].astype(F32)
    pair = jnp.concatenate([grad, pltpu.roll(grad, BAL, 1)], axis=0).astype(BF16)
    rx = {}
    for h, (first, n) in enumerate(STREAMS):
        at = pl.ds(first, n)
        for o in (2, 1, 3):
            part = own_part[h, o] + terms(up_sib[xpeer(o)], pair, first, n)
            xb[o, :, at] = part.astype(BF16)
            rx[h, o] = send(
                xb.at[o, :, at], xr.at[o, :, at], rxs.at[h, o], rxr.at[h, o], device(z, xpeer(o), y, c)
            )
    for h, (first, n) in enumerate(STREAMS):
        own_ref[:, pl.ds(first, n)] = own_part[h, 0] + terms(up_sib[x], pair, first, n)

    for copy in cz:
        copy.wait_recv()
    held = cmr[...].reshape(TOKENS, 128)
    wt_hi, wt_lo = split2(corner_weights(held.astype(F32), FEAT, TOKENS))
    from_cot = (dot(held, wt_hi, TN) + dot(held, wt_lo, TN))[:FEAT]

    ry = {}
    for h, (first, n) in enumerate(STREAMS):
        at = pl.ds(first, n)
        for o in (2, 1, 3):
            rx[h, o].wait_recv()
        total = xr[1, :, at].astype(F32) + xr[3, :, at].astype(F32)
        own_ref[:, at] = own_ref[:, at] + (total + xr[2, :, at].astype(F32))
        for m in Y_FAR:
            yb[m, at] = own_ref[ypeer(m), at].astype(BF16)
            ry[h, m] = send(
                yb.at[m, at], yr.at[m, at], rys.at[h, m], ryr.at[h, m], device(z, x, ypeer(m), c)
            )
    tau = iota((CAP, TOKENS), 1)
    rank = NZ * (tau & (BAL - 1)) + (tau >> 6)
    here = iota((CAP, TOKENS), 0)
    pick = jnp.where((rank - off == here) & (here < own_rows), 1.0, 0.0).astype(BF16)
    live_cot = jnp.where(iota((CAP, FEAT), 0) < own_rows, cot_ref[...].astype(F32), 0.0)
    gz = []
    for h, (first, n) in enumerate(STREAMS):
        at = pl.ds(first, n)
        for m in Y_ORDER:
            ry[h, m].wait_recv()
        branch = own_ref[y, at]
        for m in range(1, NY):
            branch = branch + yr[m, at].astype(F32)
        gb[at] = branch.astype(BF16)
        gz += [
            send(gb.at[at], gr.at[z, at], gzs.at[h, o], gzr.at[h, o], device(zpeer(o), x, y, c))
            for o in z_order
        ]
    gr[z] = gb[...]
    for copy in sent:
        copy.wait_send()
    for copy in gz:
        copy.wait_recv()

    first = iota((HALF, 128), 1) < BAL
    tiles = []
    for e in range(0, NZ, 2):
        g0, g1 = gr[e].astype(F32), gr[e + 1].astype(F32)
        top = jnp.where(first, g0, pltpu.roll(g1, BAL, 1))
        bottom = jnp.where(first, pltpu.roll(g0, BAL, 1), g1)
        tiles.append(jnp.concatenate([top, bottom], axis=0).astype(BF16))
    grads = jnp.concatenate(tiles, axis=1)
    gp_ref[...] = live_cot + dot(pick, grads, NT)
    gt_ref[...] = from_cot + (dot(grads, wt_hi) + dot(grads, wt_lo))


def copy_out(a_ref, b_ref, a_out, b_out):
    a_out[...] = a_ref[...]
    b_out[...] = b_ref[...]


def shards(patches, table, row_anchor, row_frac, group_rows, up_weight, down_weight, cotangent):
    vmem = pl.BlockSpec(memory_space=pltpu.VMEM)
    hbm = pl.BlockSpec(memory_space=pltpu.HBM)
    sems = lambda *n: pltpu.SemaphoreType.DMA(n)
    grad_patches, grad_table = pl.pallas_call(
        kernel,
        name="branch_grad",
        out_shape=(
            jax.ShapeDtypeStruct((CAP, FEAT), F32),
            jax.ShapeDtypeStruct((FEAT, CELLS), F32),
        ),
        in_specs=[hbm] * 8,
        out_specs=(vmem, vmem),
        scratch_shapes=[
            pltpu.SMEM((NZ,), jnp.int32),
            pltpu.VMEM((CAP, FEAT), BF16),
            pltpu.VMEM((CAP, FEAT), BF16),
            pltpu.VMEM((FEAT, CELLS), F32),
            pltpu.VMEM((2, CAP), jnp.int32),
            pltpu.VMEM((2, CAP), F32),
            pltpu.VMEM((NX, NY, NC, 2, HALF, HID), BF16),
            pltpu.VMEM((HID, D), BF16),
            pltpu.VMEM((NZ, PACK, 256), BF16),
            pltpu.VMEM((NZ, PACK, 256), BF16),
            pltpu.VMEM((BAL, 128), BF16),
            pltpu.VMEM((NZ, BAL, 128), BF16),
            pltpu.VMEM((NX, NY, NC, FEAT, 128), BF16),
            pltpu.VMEM((NX, NY, 2, HALF, HID), BF16),
            pltpu.VMEM((HID, 128), BF16),
            pltpu.VMEM((HID, 128), BF16),
            pltpu.VMEM((NX, NY, HALF, 128), BF16),
            pltpu.VMEM((NX, NY, HALF, 128), BF16),
            pltpu.VMEM((NY, HALF, 128), BF16),
            pltpu.VMEM((NY, HALF, 128), BF16),
            pltpu.VMEM((HALF, 128), BF16),
            pltpu.VMEM((NZ, HALF, 128), BF16),
            pltpu.VMEM((NY, HALF, 128), F32),
            sems(8),
            sems(NZ), sems(NZ), sems(NZ), sems(NZ),
            sems(NY), sems(NY), sems(NX, NY), sems(NX, NY), sems(NY), sems(NY), sems(1), sems(1), sems(1), sems(1),
            sems(3, NX), sems(3, NX), sems(3, NY), sems(3, NY),
            sems(3, NZ), sems(3, NZ),
        ],
        compiler_params=pltpu.CompilerParams(
            collective_id=0, has_side_effects=True, vmem_limit_bytes=60 * 2**20
        ),
    )(
        group_rows, patches, cotangent, table.T, row_anchor.T, row_frac.T,
        up_weight.reshape(NX, NY, NC, 2, HALF, HID), down_weight,
    )
    grad_patches, grad_table = pl.pallas_call(
        copy_out,
        name="copy_out",
        out_shape=(
            jax.ShapeDtypeStruct((CAP, FEAT), F32),
            jax.ShapeDtypeStruct((FEAT, CELLS), F32),
        ),
        in_specs=[vmem] * 2,
        out_specs=(vmem, vmem),
    )(grad_patches, grad_table)
    return grad_patches, grad_table.T


def solution(mesh):
    in_specs = (
        P("dp", "mp"),
        P(None, "mp"),
        P("dp", None),
        P("dp", None),
        P(),
        P(None, "mp"),
        P("mp", None),
        P("dp", "mp"),
    )
    out_specs = (P("dp", "mp"), P(None, "mp"))
    return jax.shard_map(shards, mesh=mesh, in_specs=in_specs, out_specs=out_specs, check_vma=False)
```

```python
import jax
import jax.numpy as jnp
from jax import lax
from jax.experimental import pallas as pl
from jax.experimental.pallas import tpu as pltpu
from jax.sharding import PartitionSpec as P

MESH = pl.DeviceIdType.MESH
F32, BF16 = jnp.float32, jnp.bfloat16
GRID, CELLS, D, FF = 16, 256, 6144, 24576
NZ, NX, NY, NC = 12, 4, 8, 2
NMP = NX * NY * NC
CAP, BAL, TOKENS = 192, 64, 768
FEAT, HID = D // NMP, FF // NMP
PACK = CAP // NZ
HALF = FEAT // 2
BLOCK = NX * 2 * NC * FEAT
Y_ORDER = (1, 7, 4, 3, 5, 2, 6)
Y_FAR = (4, 5, 3, 6, 2, 7, 1)
STREAMS = ((0, 16), (16, 16), (32, 16))
NN = (((1,), (0,)), ((), ()))
NT = (((1,), (1,)), ((), ()))
TN = (((0,), (0,)), ((), ()))


def dot(a, b, dims=NN):
    return lax.dot_general(a, b, dims, preferred_element_type=F32)


def iota(shape, dim):
    return lax.broadcasted_iota(jnp.int32, shape, dim)


def split2(v):
    high = v.astype(BF16)
    return high, (v - high.astype(F32)).astype(BF16)


def corner_weights(meta, first, rows):
    col = lambda k: meta[:, first + k : first + k + 1]
    a, b = col(0), col(1)
    p = (col(4) + col(3)) + col(2)
    q = (col(7) + col(6)) + col(5)
    cell = iota((rows, CELLS), 1)
    ca, cb = (cell >> 4).astype(F32), (cell & 15).astype(F32)
    wa = jnp.where(ca == a, 1.0 - p, jnp.where(ca == a + 1.0, p, 0.0))
    wb = jnp.where(cb == b, 1.0 - q, jnp.where(cb == b + 1.0, q, 0.0))
    return wa * wb


def gelu_slope(pre):
    cdf = 0.5 * (1.0 + lax.erf(pre * 0.7071067811865476))
    return cdf + pre * (jnp.exp(-0.5 * pre * pre) * 0.3989422804014327)


def kernel(
    rows_hbm, patches_hbm, cot_hbm, table_hbm, anchor_hbm, frac_hbm, up_hbm, down_hbm,
    gp_ref, gt_ref,
    rows_ref, patches_ref, cot_ref, table_ref, anchor_ref, frac_ref, up, down, msg, zin, cm, cmr, xt, up_sib, mine, theirs, xb, xr, yb, yr, gb, gr, own_ref,
    wsem, zs, zr, cs, cr, gys, gyr, gxs, gxr, gss, gsr, uss, usr, ggs, ggr, rxs, rxr, rys, ryr, gzs, gzr,
):
    z, i = lax.axis_index("dp"), lax.axis_index("mp")
    x, y, c = i // (NY * NC), (i // NC) % NY, i % NC

    def device(zz, xx, yy, cc):
        return {"dp": zz, "mp": (xx * NY + yy) * NC + cc}

    zpeer = lambda o: lax.rem(z + o, NZ)
    xpeer = lambda o: lax.rem(x + o, NX)
    ypeer = lambda o: lax.rem(y + o, NY)
    sibling = device(z, x, y, 1 - c)
    sent = []

    def send(src, dst, ssem, rsem, dev):
        copy = pltpu.make_async_remote_copy(
            src_ref=src, dst_ref=dst, send_sem=ssem, recv_sem=rsem, device_id=dev, device_id_type=MESH
        )
        copy.start()
        sent.append(copy)
        return copy

    barrier = pltpu.get_barrier_semaphore()
    peers = [device(zpeer(o), x, y, c) for o in (6, 5, 7, 4, 8, 3, 9, 2, 10, 1, 11)]
    peers += [device(z, x, ypeer(m), c) for m in Y_ORDER]
    peers += [device(z, xpeer(o), y, c) for o in (2, 1, 3)] + [sibling]
    for dev in peers:
        pl.semaphore_signal(barrier, inc=1, device_id=dev, device_id_type=MESH)

    loads = [
        pltpu.make_async_copy(src, dst, wsem.at[k])
        for k, (src, dst) in enumerate((
            (rows_hbm, rows_ref), (anchor_hbm, anchor_ref), (frac_hbm, frac_ref), (patches_hbm, patches_ref),
            (table_hbm, table_ref), (cot_hbm, cot_ref), (up_hbm, up), (down_hbm, down),
        ))
    ]
    for load in loads:
        load.start()
    for load in loads[:6]:
        load.wait()

    starts, count = [], jnp.int32(0)
    for g in range(NZ):
        starts.append(count)
        count = count + rows_ref[g]
    off = jnp.int32(0)
    for g in range(NZ):
        off = jnp.where(z == g, starts[g], off)
    own_rows = rows_ref[z]

    rho = iota((CAP, CAP), 0)
    turn = (rho >> 4) - lax.rem(off, NZ)
    slot = jnp.where(turn < 0, turn + NZ, turn) + NZ * (rho & (PACK - 1))
    perm = jnp.where(iota((CAP, CAP), 1) == slot, 1.0, 0.0).astype(BF16)

    a, b = anchor_ref[0:1, :].astype(F32), anchor_ref[1:2, :].astype(F32)
    parts = [a, b]
    for k in range(2):
        v = frac_ref[k : k + 1, :]
        for _ in range(3):
            part = v.astype(BF16).astype(F32)
            parts.append(part)
            v = v - part
    line = iota((128 - FEAT, CAP), 0)
    meta = jnp.zeros((128 - FEAT, CAP), F32)
    for k, part in enumerate(parts):
        meta = jnp.where(line == k, part, meta)
    meta = jnp.concatenate([jnp.zeros((FEAT, CAP), BF16), meta.astype(BF16)], axis=0)
    meta_rows = dot(perm, meta, NT)

    w_hi, w_lo = split2(corner_weights(meta_rows, FEAT, CAP))
    t_hi, t_lo = split2(table_ref[...])
    interp = dot(w_hi, t_hi, NT) + (dot(w_hi, t_lo, NT) + dot(w_lo, t_hi, NT))
    inputs = (dot(perm, patches_ref[...]) + interp).astype(BF16)
    msg[:, :, 0:128] = jnp.zeros((NZ, PACK, 128), BF16)
    msg[:, :, 0:FEAT] = inputs.reshape(NZ, PACK, FEAT)
    msg[:, :, 128:256] = meta_rows.astype(BF16).reshape(NZ, PACK, 128)
    msg[:, :, 128 : 128 + FEAT] = dot(perm, cot_ref[...]).astype(BF16).reshape(NZ, PACK, FEAT)

    pl.semaphore_wait(barrier, len(peers))

    z_order = (6, 5, 7, 4, 8, 3, 9, 2, 10, 1, 11)
    zc = [
        send(msg.at[zpeer(o)], zin.at[z], zs.at[o], zr.at[o], device(zpeer(o), x, y, c))
        for o in z_order
    ]
    zin[z] = msg[z]
    us = send(up_hbm.at[:, :, 1 - c], up_sib, uss.at[0], usr.at[0], sibling)

    lane = iota((1, CAP), 1)
    group, j = lane >> 4, lane & (PACK - 1)
    place = jnp.zeros((1, CAP), jnp.int32)
    for g in range(NZ):
        o12, q12 = lax.rem(starts[g], NZ), lax.div(starts[g], NZ)
        turn = z - o12
        s = jnp.where(turn < 0, turn + NZ, turn) + NZ * j
        k = q12 + j + jnp.where(turn < 0, 1, 0)
        place = jnp.where(group == g, jnp.where(s < rows_ref[g], k, -1), place)
    compact = jnp.where(iota((BAL, CAP), 0) == place, 1.0, 0.0).astype(BF16)

    for copy in zc:
        copy.wait_recv()
    rows = dot(compact, zin[...].reshape(CAP, 256))
    both = jnp.concatenate([rows[:, :128], rows[:, 128:]], axis=0)
    xt[x, y, c] = both.T[:FEAT].astype(BF16)

    def chunk(m):
        return xt.at[x, ypeer(NY - m), c]

    def to_x(m):
        return [
            send(chunk(m), chunk(m), gxs.at[o, m], gxr.at[o, m], device(z, xpeer(o), y, c))
            for o in (2, 1, 3)
        ]

    def to_sibling(m):
        line = xt.at[:, ypeer(NY - m), c]
        return send(line, line, gss.at[m], gsr.at[m], sibling)

    gy = {
        m: send(chunk(0), chunk(0), gys.at[m], gyr.at[m], device(z, x, ypeer(m), c))
        for m in Y_ORDER
    }
    gx = {0: to_x(0)}
    cm[...] = rows[:, 128:].astype(BF16)
    cmr[z] = cm[...]
    for m in Y_ORDER:
        gy[m].wait_recv()
        gx[m] = to_x(m)
    cz = [
        send(cm, cmr.at[z], cs.at[o], cr.at[o], device(zpeer(o), x, y, c)) for o in z_order
    ]
    for load in loads[6:]:
        load.wait()

    def products(pair):
        block = xt[:, pl.ds(2 * pair, 2)].reshape(BLOCK, 128)
        weights = up[:, pl.ds(2 * pair, 2)].reshape(BLOCK, HID)
        width = BLOCK // NX
        columns = [
            down[:, pl.ds(pl.multiple_of(xx * (D // NX) + pair * width, 128), width)]
            for xx in range(NX)
        ]
        return dot(block, weights, TN), dot(jnp.concatenate(columns, axis=1), block)

    half, turns = y // 2, (0, 2, 3, 1)
    gs, pre, back, whole = {}, None, None, []
    arrivals = (0,) + Y_ORDER
    for n, m in enumerate(arrivals):
        for copy in gx[m]:
            copy.wait_recv()
        gs[m] = to_sibling(m)
        for t in {3: (0,), 6: (1,), 7: (2, 3)}.get(n, ()):
            for k in arrivals[: (3, 6, 7, 8)[t]]:
                if k not in whole:
                    gs[k].wait_recv()
                    whole.append(k)
            more = products(lax.rem(half + turns[t], NY // 2))
            pre, back = more if pre is None else (pre + more[0], back + more[1])

    low = iota((HID, 128), 1) < BAL
    grad = pltpu.roll(back, BAL, 1) * gelu_slope(pre.T)
    grad = jnp.where(low, grad, 0.0)
    mine[...] = grad.astype(BF16)
    gg = send(mine, theirs, ggs.at[0], ggr.at[0], sibling)
    pair = jnp.concatenate([grad, pltpu.roll(grad, BAL, 1)], axis=0).astype(BF16)

    def terms(weights, grads, first, n):
        weights = weights[:, :, first : first + n]
        weights = jnp.concatenate([weights[:, 0], weights[:, 1]], axis=2)
        return dot(weights.reshape(NY * n, 2 * HID), grads).reshape(NY, n, 128)

    own_part = {
        (h, o): terms(up[xpeer(o), :, c], pair, *rows)
        for h, rows in enumerate(STREAMS)
        for o in (2, 1, 3, 0)
    }
    us.wait_recv()
    gg.wait_recv()
    grad = theirs[...].astype(F32)
    pair = jnp.concatenate([grad, pltpu.roll(grad, BAL, 1)], axis=0).astype(BF16)
    rx = {}
    for h, (first, n) in enumerate(STREAMS):
        at = pl.ds(first, n)
        for o in (2, 1, 3):
            part = own_part[h, o] + terms(up_sib[xpeer(o)], pair, first, n)
            xb[o, :, at] = part.astype(BF16)
            rx[h, o] = send(
                xb.at[o, :, at], xr.at[o, :, at], rxs.at[h, o], rxr.at[h, o], device(z, xpeer(o), y, c)
            )
    for h, (first, n) in enumerate(STREAMS):
        own_ref[:, pl.ds(first, n)] = own_part[h, 0] + terms(up_sib[x], pair, first, n)

    for copy in cz:
        copy.wait_recv()
    held = cmr[...].reshape(TOKENS, 128)
    wt_hi, wt_lo = split2(corner_weights(held.astype(F32), FEAT, TOKENS))
    from_cot = (dot(held, wt_hi, TN) + dot(held, wt_lo, TN))[:FEAT]

    ry = {}
    for h, (first, n) in enumerate(STREAMS):
        at = pl.ds(first, n)
        for o in (2, 1, 3):
            rx[h, o].wait_recv()
        total = xr[1, :, at].astype(F32) + xr[3, :, at].astype(F32)
        own_ref[:, at] = own_ref[:, at] + (total + xr[2, :, at].astype(F32))
        for m in Y_FAR:
            yb[m, at] = own_ref[ypeer(m), at].astype(BF16)
            ry[h, m] = send(
                yb.at[m, at], yr.at[m, at], rys.at[h, m], ryr.at[h, m], device(z, x, ypeer(m), c)
            )
    tau = iota((CAP, TOKENS), 1)
    rank = NZ * (tau & (BAL - 1)) + (tau >> 6)
    here = iota((CAP, TOKENS), 0)
    pick = jnp.where((rank - off == here) & (here < own_rows), 1.0, 0.0).astype(BF16)
    live_cot = jnp.where(iota((CAP, FEAT), 0) < own_rows, cot_ref[...].astype(F32), 0.0)
    gz = []
    for h, (first, n) in enumerate(STREAMS):
        at = pl.ds(first, n)
        for m in Y_ORDER:
            ry[h, m].wait_recv()
        branch = own_ref[y, at]
        for m in range(1, NY):
            branch = branch + yr[m, at].astype(F32)
        gb[at] = branch.astype(BF16)
        gz += [
            send(gb.at[at], gr.at[z, at], gzs.at[h, o], gzr.at[h, o], device(zpeer(o), x, y, c))
            for o in z_order
        ]
    gr[z] = gb[...]
    for copy in sent:
        copy.wait_send()
    for copy in gz:
        copy.wait_recv()

    first = iota((HALF, 128), 1) < BAL
    tiles = []
    for e in range(0, NZ, 2):
        g0, g1 = gr[e].astype(F32), gr[e + 1].astype(F32)
        top = jnp.where(first, g0, pltpu.roll(g1, BAL, 1))
        bottom = jnp.where(first, pltpu.roll(g0, BAL, 1), g1)
        tiles.append(jnp.concatenate([top, bottom], axis=0).astype(BF16))
    grads = jnp.concatenate(tiles, axis=1)
    gp_ref[...] = live_cot + dot(pick, grads, NT)
    gt_ref[...] = from_cot + (dot(grads, wt_hi) + dot(grads, wt_lo))


def copy_out(a_ref, b_ref, a_out, b_out):
    a_out[...] = a_ref[...]
    b_out[...] = b_ref[...]


def shards(patches, table, row_anchor, row_frac, group_rows, up_weight, down_weight, cotangent):
    vmem = pl.BlockSpec(memory_space=pltpu.VMEM)
    hbm = pl.BlockSpec(memory_space=pltpu.HBM)
    sems = lambda *n: pltpu.SemaphoreType.DMA(n)
    grad_patches, grad_table = pl.pallas_call(
        kernel,
        name="branch_grad",
        out_shape=(
            jax.ShapeDtypeStruct((CAP, FEAT), F32),
            jax.ShapeDtypeStruct((FEAT, CELLS), F32),
        ),
        in_specs=[hbm] * 8,
        out_specs=(vmem, vmem),
        scratch_shapes=[
            pltpu.SMEM((NZ,), jnp.int32),
            pltpu.VMEM((CAP, FEAT), BF16),
            pltpu.VMEM((CAP, FEAT), BF16),
            pltpu.VMEM((FEAT, CELLS), F32),
            pltpu.VMEM((2, CAP), jnp.int32),
            pltpu.VMEM((2, CAP), F32),
            pltpu.VMEM((NX, NY, NC, 2, HALF, HID), BF16),
            pltpu.VMEM((HID, D), BF16),
            pltpu.VMEM((NZ, PACK, 256), BF16),
            pltpu.VMEM((NZ, PACK, 256), BF16),
            pltpu.VMEM((BAL, 128), BF16),
            pltpu.VMEM((NZ, BAL, 128), BF16),
            pltpu.VMEM((NX, NY, NC, FEAT, 128), BF16),
            pltpu.VMEM((NX, NY, 2, HALF, HID), BF16),
            pltpu.VMEM((HID, 128), BF16),
            pltpu.VMEM((HID, 128), BF16),
            pltpu.VMEM((NX, NY, HALF, 128), BF16),
            pltpu.VMEM((NX, NY, HALF, 128), BF16),
            pltpu.VMEM((NY, HALF, 128), BF16),
            pltpu.VMEM((NY, HALF, 128), BF16),
            pltpu.VMEM((HALF, 128), BF16),
            pltpu.VMEM((NZ, HALF, 128), BF16),
            pltpu.VMEM((NY, HALF, 128), F32),
            sems(8),
            sems(NZ), sems(NZ), sems(NZ), sems(NZ),
            sems(NY), sems(NY), sems(NX, NY), sems(NX, NY), sems(NY), sems(NY), sems(1), sems(1), sems(1), sems(1),
            sems(3, NX), sems(3, NX), sems(3, NY), sems(3, NY),
            sems(3, NZ), sems(3, NZ),
        ],
        compiler_params=pltpu.CompilerParams(
            collective_id=0, has_side_effects=True, vmem_limit_bytes=60 * 2**20
        ),
    )(
        group_rows, patches, cotangent, table.T, row_anchor.T, row_frac.T,
        up_weight.reshape(NX, NY, NC, 2, HALF, HID), down_weight,
    )
    grad_patches, grad_table = pl.pallas_call(
        copy_out,
        name="copy_out",
        out_shape=(
            jax.ShapeDtypeStruct((CAP, FEAT), F32),
            jax.ShapeDtypeStruct((FEAT, CELLS), F32),
        ),
        in_specs=[vmem] * 2,
        out_specs=(vmem, vmem),
    )(grad_patches, grad_table)
    return grad_patches, grad_table.T


def solution(mesh):
    in_specs = (
        P("dp", "mp"),
        P(None, "mp"),
        P("dp", None),
        P("dp", None),
        P(),
        P(None, "mp"),
        P("mp", None),
        P("dp", "mp"),
    )
    out_specs = (P("dp", "mp"), P(None, "mp"))
    return jax.shard_map(shards, mesh=mesh, in_specs=in_specs, out_specs=out_specs, check_vma=False)
```
